32 devices in a mesh: groups: 2 (over x), dp: 2 (over core), expert: 8 (over z, y).
Axes of the slice: x: 2, y: 2, z: 4, core: 2. Of those that a mesh axis runs over, the one named last changes fastest.
Arguments:
- tokens: bfloat16 [1024, 7168], P(('groups', 'dp', 'expert')), parts along dimension 0, may hold values from -6 to 6
- routes: int32 [1024, 4], P(('groups', 'dp', 'expert')), parts along dimension 0, may hold values from 0 to 7, all different within a row; in each aligned block of 32 rows (0 to 31, 32 to 63, ...) at most 32 rows name the same one
- gate_weights: float32 [1024, 4], P(('groups', 'dp', 'expert')), parts along dimension 0, may hold values from 0.05 to 0.6
- w_gate: bfloat16 [8, 7168, 1024], P('expert', None, 'dp'), may hold values from -0.0625 to 0.0625
- w_up: bfloat16 [8, 7168, 1024], P('expert', None, 'dp'), may hold values from -0.0625 to 0.0625
- w_down: bfloat16 [8, 1024, 7168], P('expert', 'dp'), may hold values from -0.1875 to 0.1875
Outputs:
- layer_out: bfloat16 [1024, 7168], P(('groups', 'dp', 'expert')), parts along dimension 0
The draws below stay inside these ranges and needn't reach their ends.
There are 2 independent parts, one for each index of `groups`. The reference program is written for one: setup_inputs(seed, part) draws one part's arguments, and reference() takes and returns one part's arrays. A program takes and returns all parts, laid end to end along the dimension named above; an argument that names none is the same for every part. Nothing has to cross between parts.
Inputs may be any that keep to these rules, and one draw needn't show every extreme that they name: `routes`: each row names 4 different experts. Among the rows of one device (aligned blocks of 32 rows) no expert is named more than 32 times, a bound that some block reaches.
All inputs are finite; a program needn't handle non-finite values.
Results may differ from the reference program's by a relative error of at most 0.0085.
Values may be sent and summed in bfloat16 or wider, within the bound.
A program may use at most 128 MiB of HBM per device.

```python
import math
import jax
import jax.numpy as jnp
import numpy as np
from jax import lax

D = 7168
FF = 1024
TOP = 4
TOK_DEV = 32
EXPERTS = 8
FF_DEV = 512
CAP = 32
TOKENS = 512
N_DP = 2
N_EXPERT = 8


def block_scale(own_key, extent, pieces, low, high):
    level = 1.0
    for axis_at, shards_of in pieces:
        draws = jax.random.uniform(jax.random.fold_in(jax.random.fold_in(own_key, 6), axis_at), (shards_of,), jnp.float32, low / len(pieces), high / len(pieces))
        level = level * jnp.repeat(jnp.exp(draws), extent[axis_at] // shards_of).reshape((-1,) + (1,) * (len(extent) - 1 - axis_at))
    return level


def shared_out(key, own, number, rows, count, top, limit, lean):
    sequence = jax.random.permutation(key, count)
    heavy_load, usual = shares(count, rows * top, limit, lean, True), shares(count, rows * top, limit, lean, False)
    places = jnp.arange(count)

    def named(sizes, offset_by):
        used = int((sizes > 0).sum())
        fixed = max(1, used // 4)
        moved = fixed + (places - fixed + offset_by * (used - fixed)) % max(1, count - fixed)
        return jnp.zeros((count,), jnp.int32).at[sequence[jnp.where(places < fixed, places, moved)]].set(jnp.asarray(sizes, jnp.int32))

    sizes = jnp.where(number % 4 == 0, named(heavy_load, number // 4), named(usual, number - number // 4 - 1))
    mixed = jax.random.permutation(jax.random.fold_in(own, 3), count)
    donor, taker = mixed[0:count // 2 * 2:2], mixed[1:count // 2 * 2:2]
    slack = jnp.minimum(sizes[donor] - 1, limit - sizes[taker]) // 2
    slack = jnp.where((donor == sequence[0]) | (taker == sequence[0]) | (sizes[taker] == 0), 0, jnp.maximum(slack, 0))
    moved = jax.random.randint(jax.random.fold_in(own, 4), (count // 2,), 0, 1 << 20) % (slack + 1)
    sizes = sizes.at[donor].add(-moved).at[taker].add(moved)
    members = jnp.searchsorted(jnp.cumsum(sizes), jnp.arange(rows * top), side="right").astype(jnp.int32)
    grid = members.reshape(top, rows).T
    grid = grid[jax.random.permutation(jax.random.fold_in(own, 1), rows)]
    offset_by = jax.random.randint(jax.random.fold_in(own, 2), (rows, 1), 0, top)
    return jnp.take_along_axis(grid, (jnp.arange(top)[None, :] + offset_by) % top, axis=1)


def shares(number_of, total, limit, skew, full):
    loads = [(1 << 20) // math.isqrt(standing ** skew) + 1 for standing in range(1, number_of + 1)]
    largest = limit if full else min(limit, max(-(-total // number_of), total * loads[0] // sum(loads)))
    least = 1 if total - largest >= number_of - 1 else 0
    holding, rest = [largest] + [least] * (number_of - 1), total - largest - least * (number_of - 1)
    while rest > 0:
        free = [i for i in range(1, number_of) if holding[i] < largest] or [i for i in range(1, number_of) if holding[i] < limit]
        mass, remaining = sum([loads[i] for i in free]), rest
        for i in free:
            more = min(limit - holding[i], max(1, remaining * loads[i] // mass), rest)
            holding[i] = holding[i] + more
            rest = rest - more
    return np.array(holding)


def gaussian(key, extent, width, most, pieces=(), held_as=jnp.bfloat16):
    level = block_scale(key, extent, pieces, -0.22, 0.18) if pieces else 1.0
    entries = jax.random.normal(key, extent, jnp.float32) * width * level
    return jnp.minimum(jnp.maximum(entries, -most), most).astype(held_as)


def setup_inputs(seed: int = 0, part: int = 0) -> dict:
    keys = jax.random.split(jax.random.key(seed), 7)
    part_keys = jax.random.split(jax.random.fold_in(keys[6], part), 7)
    tokens = gaussian(part_keys[0], (TOKENS, D), 1.0, 6.0, ((0, 16),))
    routes_keys = jax.random.split(jax.random.fold_in(part_keys[1], 1), TOKENS // TOK_DEV)
    routes_turns = jax.random.permutation(jax.random.fold_in(part_keys[1], 3), TOKENS // TOK_DEV)
    routes = jax.vmap(lambda own, number: shared_out(jax.random.fold_in(part_keys[1], 2), own, number, TOK_DEV, EXPERTS, TOP, CAP, 2))(routes_keys, routes_turns).reshape((TOKENS, TOP))
    gate_weights = jnp.clip(jnp.exp(math.log(0.6) - 2.4849067 * jax.random.uniform(part_keys[2], (TOKENS, TOP), jnp.float32) ** block_scale(part_keys[2], (TOKENS, TOP), ((0, 16),), -0.2, 0.2)), 0.05, 0.6)
    w_gate = gaussian(keys[3], (EXPERTS, D, FF), D ** -0.5, 0.0625, ((0, 8), (2, 2)))
    w_up = gaussian(keys[4], (EXPERTS, D, FF), D ** -0.5, 0.0625, ((0, 8), (2, 2)))
    w_down = gaussian(keys[5], (EXPERTS, FF, D), FF ** -0.5, 0.1875, ((0, 8), (1, 2)))
    return {"tokens": tokens, "routes": routes, "gate_weights": gate_weights, "w_gate": w_gate, "w_up": w_up, "w_down": w_down}


def reference(tokens, routes, gate_weights, w_gate, w_up, w_down):
    route_count = TOKENS * TOP
    max_rows = N_DP * N_EXPERT * CAP
    flat_exp = routes.reshape(-1).astype(jnp.int32)
    flat_tok = (jnp.arange(route_count, dtype=jnp.int32) // TOP).astype(jnp.int32)
    flat_gate = gate_weights.reshape(-1)

    def one_expert(totals, expert):
        key_flags = (flat_exp != expert).astype(jnp.int32)
        order_idx = jnp.argsort(key_flags, stable=True)[:max_rows].astype(jnp.int32)
        is_valid = flat_exp[order_idx] == expert
        token_ids = flat_tok[order_idx]
        row_data = tokens[token_ids]
        gate_out = jnp.dot(row_data, w_gate[expert], preferred_element_type=jnp.float32)
        up_out = jnp.dot(row_data, w_up[expert], preferred_element_type=jnp.float32)
        hidden = (jax.nn.silu(gate_out) * up_out).astype(jnp.bfloat16)
        down_mat = w_down[expert]
        routed = jnp.zeros((max_rows, D), jnp.float32)
        for block_index in range(N_DP):
            start_col = block_index * FF_DEV
            partial_out = jnp.dot(hidden[:, start_col:start_col + FF_DEV], down_mat[start_col:start_col + FF_DEV], preferred_element_type=jnp.float32)
            rounded = lax.optimization_barrier(partial_out.astype(jnp.bfloat16))
            routed = routed + rounded.astype(jnp.float32)
        weight = jnp.where(is_valid, flat_gate[order_idx], 0.0).astype(jnp.float32)
        totals = totals + jax.ops.segment_sum(routed * weight[:, None], token_ids, num_segments=TOKENS)
        return totals, None

    totals, unused = lax.scan(one_expert, jnp.zeros((TOKENS, D), jnp.float32), jnp.arange(EXPERTS, dtype=jnp.int32))
    return totals.astype(jnp.bfloat16)
```

```python
import functools

import jax
import jax.numpy as jnp
from jax import lax
from jax.experimental import pallas as pl
from jax.experimental.pallas import tpu as pltpu
from jax.sharding import PartitionSpec as P

MESH = pl.DeviceIdType.MESH
LANES = 128


def ring_place(n, expert):
    if n != 8:
        return expert
    return lax.select(lax.rem(expert, 2) == 0, expert // 2, (2 * n - 1 - expert) // 2)


def ring_expert(n, place):
    if n != 8:
        return place
    return lax.select(place < n // 2, 2 * place, 2 * n - 1 - 2 * place)


def kernel(n, tokens, routes, gates, w_gate, w_up, w_down, out,
           x, mine, theirs, back, wg, wu, wd, hid,
           w_sem, fwd_send, fwd_recv, pair_send, pair_recv, sum_send, sum_recv, back_send, back_recv):
    rows, width = tokens.shape
    top = routes.shape[1]
    ffd = wg.shape[1]
    half, sub = n // 2, rows // 2
    expert = lax.axis_index("expert")
    core = lax.axis_index("dp")
    place = ring_place(n, expert)
    nxt = ring_expert(n, lax.rem(place + 1, n))
    prv = ring_expert(n, lax.rem(place + n - 1, n))
    ahead, partner = ({"expert": nxt}, {"expert": prv}), {"dp": 1 - core}

    def slot(d, s):
        return 0 if s == 0 else n - 1 if s == half else 2 * s - 1 + d

    def rdma(src, dst, send, recv, device):
        return pltpu.make_async_remote_copy(
            src_ref=src, dst_ref=dst, send_sem=send, recv_sem=recv, device_id=device, device_id_type=MESH)

    loads = [pltpu.make_async_copy(src.at[0], dst, w_sem.at[i])
             for i, (src, dst) in enumerate(((w_gate, wg), (w_up, wu), (w_down, wd)))]
    for load in loads:
        load.start()

    barrier = pltpu.get_barrier_semaphore()
    for device in (*ahead, partner):
        pl.semaphore_signal(barrier, inc=1, device_id=device, device_id_type=MESH)

    x[0:rows, 0:width] = tokens[...]
    lane = lax.broadcasted_iota(jnp.int32, (rows, LANES), 1)
    left = jnp.zeros((rows, LANES), jnp.float32)
    for k in range(top):
        for part in range(3):
            left = left + jnp.where(lane == routes[:, k:k + 1] + part * n, gates[:, k:k + 1], 0.0)
    high = left.astype(jnp.bfloat16).astype(jnp.float32)
    mid = (left - high).astype(jnp.bfloat16).astype(jnp.float32)
    low = left - high - mid
    x[0:rows, width:width + LANES] = jnp.where(lane < n, high, jnp.where(lane < 2 * n, mid, low)).astype(jnp.bfloat16)
    pl.semaphore_wait(barrier, 3)

    def forward(d, s, c):
        a, b = slot(d, s) * 2 * rows + c * sub, slot(d, s + 1) * 2 * rows + c * sub
        return rdma(x.at[pl.ds(a, sub)], x.at[pl.ds(b, sub)],
                    fwd_send.at[d, s, c], fwd_recv.at[d, s + 1, c], ahead[d])

    def pair(b):
        return rdma(x.at[pl.ds(b * 2 * rows, rows)], x.at[pl.ds(b * 2 * rows + rows, rows)],
                    pair_send.at[b], pair_recv.at[b], partner)

    def summed(b):
        return rdma(x.at[pl.ds(b * 2 * rows + rows, rows), pl.ds(0, width)], theirs.at[pl.ds(b * rows, rows)],
                    sum_send.at[b], sum_recv.at[b], partner)

    sent = []

    def start(copy):
        copy.start()
        sent.append(copy)

    def compute(first, blocks):
        base, count = first * 2 * rows, blocks * 2 * rows
        span = pl.ds(base, count)
        tile = min(256, ffd)

        def up(j, _):
            cols = pl.ds(pl.multiple_of(j * tile, tile), tile)
            g = jnp.dot(x[span, 0:width], wg[:, cols], preferred_element_type=jnp.float32)
            u = jnp.dot(x[span, 0:width], wu[:, cols], preferred_element_type=jnp.float32)
            hid[0:count, cols] = (g / (1.0 + jnp.exp(-g)) * u).astype(jnp.bfloat16)
            return 0

        lax.fori_loop(0, ffd // tile, up, 0)
        lane = lax.broadcasted_iota(jnp.int32, (count, LANES), 1)
        own = (lane == expert) | (lane == expert + n) | (lane == expert + 2 * n)
        weight = jnp.sum(jnp.where(own, x[span, width:width + LANES].astype(jnp.float32), 0.0), axis=1, keepdims=True)
        wide = 512 if width % 512 == 0 else LANES

        def down(j, _):
            cols = pl.ds(pl.multiple_of(j * wide, wide), wide)
            y = jnp.dot(hid[0:count, :], wd[:, cols], preferred_element_type=jnp.float32)
            y = (y * weight).astype(jnp.bfloat16)
            for i in range(blocks):
                at = i * 2 * rows
                mine[(first + i) * rows:(first + i + 1) * rows, cols] = y[at:at + rows]
                x[base + at + rows:base + at + 2 * rows, cols] = y[at + rows:at + 2 * rows]
            return 0

        lax.fori_loop(0, width // wide, down, 0)
        for i in range(blocks):
            start(summed(first + i))

    for c in (0, 1):
        for d in (0, 1):
            start(forward(d, 0, c))
    start(pair(0))
    for s in range(1, half):
        for c in (0, 1):
            for d in (0, 1):
                forward(d, s - 1, c).wait_recv()
                if s < half - 1 or c == d:
                    start(forward(d, s, c))
        for d in (0, 1):
            start(pair(slot(d, s)))
        if s == 1:
            for load in loads:
                load.wait()
            pair(0).wait_recv()
            compute(0, 1)
        for d in (0, 1):
            pair(slot(d, s)).wait_recv()
        compute(slot(0, s), 2)

    def home(d, s, c):
        at = slot(1 - d, s) * rows + c * sub
        from_ = mine.at[pl.ds(at, sub)] if s == (half if c != d else half - 1) else back.at[pl.ds((d * half + s) * rows + c * sub, sub)]
        return rdma(from_, back.at[pl.ds((d * half + s - 1) * rows + c * sub, sub)],
                    back_send.at[d, s, c], back_recv.at[d, s - 1, c], ahead[d])

    wide = 1024 if width % 1024 == 0 else LANES

    def step(d, s, c, last):
        at = slot(1 - d, s) * rows + c * sub
        if not last:
            home(d, s + 1, c).wait_recv()
        here = (d * half + s) * rows + c * sub

        def add(j, _):
            cols = pl.ds(pl.multiple_of(j * wide, wide), wide)
            total = mine[at:at + sub, cols].astype(jnp.float32) + theirs[at:at + sub, cols].astype(jnp.float32)
            if last:
                mine[at:at + sub, cols] = total.astype(jnp.bfloat16)
            else:
                total = total + back[here:here + sub, cols].astype(jnp.float32)
                back[here:here + sub, cols] = total.astype(jnp.bfloat16)
            return 0

        lax.fori_loop(0, width // wide, add, 0)
        start(home(d, s, c))

    def finish(c):
        for d in (0, 1):
            home(d, 1, c).wait_recv()
        a, b, t = c * sub, half * rows + c * sub, c * sub

        def add(j, _):
            cols = pl.ds(pl.multiple_of(j * wide, wide), wide)
            total = mine[t:t + sub, cols].astype(jnp.float32) + theirs[t:t + sub, cols].astype(jnp.float32)
            total = total + back[a:a + sub, cols].astype(jnp.float32) + back[b:b + sub, cols].astype(jnp.float32)
            out[t:t + sub, cols] = total.astype(jnp.bfloat16)
            return 0

        lax.fori_loop(0, width // wide, add, 0)

    for b in range(n - 1):
        summed(b).wait_recv()
    for d in (0, 1):
        step(d, half - 1, d, True)
    for d in (0, 1):
        forward(d, half - 1, d).wait_recv()
    start(pair(n - 1))
    pair(n - 1).wait_recv()
    compute(n - 1, 1)
    summed(n - 1).wait_recv()
    for d in (0, 1):
        step(d, half, 1 - d, True)
    for i in range(1, half):
        for d in (0, 1):
            if half - 1 - i > 0:
                step(d, half - 1 - i, d, False)
        for d in (0, 1):
            step(d, half - i, 1 - d, False)
    for c in (0, 1):
        finish(c)
    for copy in sent:
        copy.wait_send()


def local(tokens, routes, gate_weights, w_gate, w_up, w_down):
    rows, width = tokens.shape
    n = lax.axis_size("expert")
    half, ffd = n // 2, w_gate.shape[2]
    bf = jnp.bfloat16
    dma = pltpu.SemaphoreType.DMA
    vmem, anyw = pl.BlockSpec(memory_space=pltpu.VMEM), pl.BlockSpec(memory_space=pl.ANY)
    return pl.pallas_call(
        functools.partial(kernel, n),
        out_shape=jax.ShapeDtypeStruct((rows, width), bf),
        in_specs=[vmem, vmem, vmem, anyw, anyw, anyw],
        out_specs=vmem,
        scratch_shapes=[
            pltpu.VMEM((2 * n * rows, width + LANES), bf),
            pltpu.VMEM((n * rows, width), bf),
            pltpu.VMEM((n * rows, width), bf),
            pltpu.VMEM((n * rows, width), bf),
            pltpu.VMEM((width, ffd), bf),
            pltpu.VMEM((width, ffd), bf),
            pltpu.VMEM((ffd, width), bf),
            pltpu.VMEM((4 * rows, ffd), bf),
            dma((3,)),
            dma((2, half + 1, 2)), dma((2, half + 1, 2)),
            dma((n,)), dma((n,)),
            dma((n,)), dma((n,)),
            dma((2, half + 1, 2)), dma((2, half + 1, 2)),
        ],
        compiler_params=pltpu.CompilerParams(
            collective_id=0, has_side_effects=True, vmem_limit_bytes=61 * 2 ** 20),
        cost_estimate=pl.CostEstimate(
            flops=12 * n * rows * width * ffd, bytes_accessed=6 * width * ffd, transcendentals=2 * n * rows * ffd),
    )(tokens, routes, gate_weights, w_gate, w_up, w_down)


def solution(mesh):
    spread = P(("groups", "dp", "expert"), None)
    return jax.shard_map(
        local,
        mesh=mesh,
        in_specs=(spread, spread, spread, P("expert", None, "dp"), P("expert", None, "dp"), P("expert", "dp", None)),
        out_specs=spread,
        check_vma=False,
    )
```

```python
import functools

import jax
import jax.numpy as jnp
from jax import lax
from jax.experimental import pallas as pl
from jax.experimental.pallas import tpu as pltpu
from jax.sharding import PartitionSpec as P

MESH = pl.DeviceIdType.MESH
LANES = 128


def ring_place(n, expert):
    if n != 8:
        return expert
    return lax.select(lax.rem(expert, 2) == 0, expert // 2, (2 * n - 1 - expert) // 2)


def ring_expert(n, place):
    if n != 8:
        return place
    return lax.select(place < n // 2, 2 * place, 2 * n - 1 - 2 * place)


def kernel(n, tokens, routes, gates, w_gate, w_up, w_down, out,
           x, mine, theirs, back, wg, wu, wd, hid,
           w_sem, fwd_send, fwd_recv, pair_send, pair_recv, sum_send, sum_recv, back_send, back_recv):
    rows, width = tokens.shape
    top = routes.shape[0]
    ffd = wg.shape[1]
    half, sub = n // 2, rows // 2
    expert = lax.axis_index("expert")
    core = lax.axis_index("dp")
    place = ring_place(n, expert)
    nxt = ring_expert(n, lax.rem(place + 1, n))
    prv = ring_expert(n, lax.rem(place + n - 1, n))
    ahead, partner = ({"expert": nxt}, {"expert": prv}), {"dp": 1 - core}

    def slot(d, s):
        return 0 if s == 0 else n - 1 if s == half else 2 * s - 1 + d

    def rdma(src, dst, send, recv, device):
        return pltpu.make_async_remote_copy(
            src_ref=src, dst_ref=dst, send_sem=send, recv_sem=recv, device_id=device, device_id_type=MESH)

    loads = [pltpu.make_async_copy(src.at[0], dst, w_sem.at[i])
             for i, (src, dst) in enumerate(((w_gate, wg), (w_up, wu), (w_down, wd)))]
    for load in loads:
        load.start()

    barrier = pltpu.get_barrier_semaphore()
    for device in (*ahead, partner):
        pl.semaphore_signal(barrier, inc=1, device_id=device, device_id_type=MESH)

    x[0:rows, 0:width] = tokens[...]
    line = lax.broadcasted_iota(jnp.int32, (LANES, rows), 0)
    left = jnp.zeros((LANES, rows), jnp.float32)
    for k in range(top):
        for part in range(3):
            left = left + jnp.where(line == routes[k:k + 1, :] + part * n, gates[k:k + 1, :], 0.0)
    high = left.astype(jnp.bfloat16).astype(jnp.float32)
    mid = (left - high).astype(jnp.bfloat16).astype(jnp.float32)
    low = left - high - mid
    parts = jnp.where(line < n, high, jnp.where(line < 2 * n, mid, low)).astype(jnp.bfloat16)
    same = lax.broadcasted_iota(jnp.int32, (rows, rows), 0) == lax.broadcasted_iota(jnp.int32, (rows, rows), 1)
    eye = jnp.where(same, 1.0, 0.0).astype(jnp.bfloat16)
    turned = lax.dot_general(eye, parts, (((1,), (1,)), ((), ())), preferred_element_type=jnp.float32)
    x[0:rows, width:width + LANES] = turned.astype(jnp.bfloat16)
    pl.semaphore_wait(barrier, 3)

    def forward(d, s, c):
        a, b = slot(d, s) * 2 * rows + c * sub, slot(d, s + 1) * 2 * rows + c * sub
        return rdma(x.at[pl.ds(a, sub)], x.at[pl.ds(b, sub)],
                    fwd_send.at[d, s, c], fwd_recv.at[d, s + 1, c], ahead[d])

    def pair(b, c):
        at = b * 2 * rows + c * sub
        return rdma(x.at[pl.ds(at, sub)], x.at[pl.ds(at + rows, sub)],
                    pair_send.at[b, c], pair_recv.at[b, c], partner)

    def summed(b, c):
        return rdma(x.at[pl.ds(b * 2 * rows + rows + c * sub, sub), pl.ds(0, width)],
                    theirs.at[pl.ds(b * rows + c * sub, sub)], sum_send.at[b, c], sum_recv.at[b, c], partner)

    sent = []

    def start(copy):
        copy.start()
        sent.append(copy)

    def compute(first, blocks):
        base, count = first * 2 * rows, blocks * 2 * rows
        span = pl.ds(base, count)
        tile = min(256, ffd)

        def up(j, _):
            cols = pl.ds(pl.multiple_of(j * tile, tile), tile)
            g = jnp.dot(x[span, 0:width], wg[:, cols], preferred_element_type=jnp.float32)
            u = jnp.dot(x[span, 0:width], wu[:, cols], preferred_element_type=jnp.float32)
            hid[0:count, cols] = (g / (1.0 + jnp.exp(-g)) * u).astype(jnp.bfloat16)
            return 0

        lax.fori_loop(0, ffd // tile, up, 0)
        lane = lax.broadcasted_iota(jnp.int32, (count, LANES), 1)
        own = (lane == expert) | (lane == expert + n) | (lane == expert + 2 * n)
        weight = jnp.sum(jnp.where(own, x[span, width:width + LANES].astype(jnp.float32), 0.0), axis=1, keepdims=True)
        wide = 1792 if width % 1792 == 0 else LANES

        def down(j, _):
            cols = pl.ds(pl.multiple_of(j * wide, wide), wide)
            y = jnp.dot(hid[0:count, :], wd[:, cols], preferred_element_type=jnp.float32)
            y = (y * weight).astype(jnp.bfloat16)
            for i in range(blocks):
                at = i * 2 * rows
                mine[(first + i) * rows:(first + i + 1) * rows, cols] = y[at:at + rows]
                x[base + at + rows:base + at + 2 * rows, cols] = y[at + rows:at + 2 * rows]
            return 0

        lax.fori_loop(0, width // wide, down, 0)
        for c in (0, 1):
            for i in range(blocks):
                start(summed(first + i, 1 - c if i == 0 else c))

    for c in (0, 1):
        for d in (0, 1):
            start(forward(d, 0, c))
            if d == 1:
                start(pair(0, c))
    for s in range(1, half):
        for c in (0, 1):
            for d in (0, 1):
                forward(d, s - 1, c).wait_recv()
                if s < half - 1 or c == d:
                    start(forward(d, s, c))
                start(pair(slot(d, s), c))
        if s == 1:
            for load in loads:
                load.wait()
            for c in (0, 1):
                pair(0, c).wait_recv()
            compute(0, 1)
        for d in (0, 1):
            for c in (0, 1):
                pair(slot(d, s), c).wait_recv()
        compute(slot(0, s), 2)

    def home(d, s, c):
        at = slot(1 - d, s) * rows + c * sub
        from_ = mine.at[pl.ds(at, sub)] if s == (half if c != d else half - 1) else back.at[pl.ds((d * half + s) * rows + c * sub, sub)]
        return rdma(from_, back.at[pl.ds((d * half + s - 1) * rows + c * sub, sub)],
                    back_send.at[d, s, c], back_recv.at[d, s - 1, c], ahead[d])

    wide = 512 if width % 512 == 0 else LANES

    def step(d, s, c, last):
        at = slot(1 - d, s) * rows + c * sub
        summed(slot(1 - d, s), c).wait_recv()
        if not last:
            home(d, s + 1, c).wait_recv()
        here = (d * half + s) * rows + c * sub

        for j in range(width // wide):
            cols = pl.ds(j * wide, wide)
            total = mine[at:at + sub, cols].astype(jnp.float32) + theirs[at:at + sub, cols].astype(jnp.float32)
            if last:
                mine[at:at + sub, cols] = total.astype(jnp.bfloat16)
            else:
                total = total + back[here:here + sub, cols].astype(jnp.float32)
                back[here:here + sub, cols] = total.astype(jnp.bfloat16)
        start(home(d, s, c))

    def finish(c):
        summed(0, c).wait_recv()
        for d in (0, 1):
            home(d, 1, c).wait_recv()
        a, b, t = c * sub, half * rows + c * sub, c * sub

        for j in range(width // wide):
            cols = pl.ds(j * wide, wide)
            total = mine[t:t + sub, cols].astype(jnp.float32) + theirs[t:t + sub, cols].astype(jnp.float32)
            total = total + back[a:a + sub, cols].astype(jnp.float32) + back[b:b + sub, cols].astype(jnp.float32)
            out[t:t + sub, cols] = total.astype(jnp.bfloat16)

    for d in (0, 1):
        step(d, half - 1, d, True)
    for d in (0, 1):
        forward(d, half - 1, d).wait_recv()
        start(pair(n - 1, d))
    for d in (0, 1):
        pair(n - 1, d).wait_recv()
    compute(n - 1, 1)
    for d in (0, 1):
        step(d, half, 1 - d, True)
    for i in range(1, half):
        for d in (0, 1):
            if half - 1 - i > 0:
                step(d, half - 1 - i, d, False)
        for d in (0, 1):
            step(d, half - i, 1 - d, False)
    for c in (0, 1):
        finish(c)
    for copy in sent:
        copy.wait_send()


def local(tokens, routes, gate_weights, w_gate, w_up, w_down):
    rows, width = tokens.shape
    n = lax.axis_size("expert")
    half, ffd = n // 2, w_gate.shape[2]
    bf = jnp.bfloat16
    dma = pltpu.SemaphoreType.DMA
    vmem, anyw = pl.BlockSpec(memory_space=pltpu.VMEM), pl.BlockSpec(memory_space=pl.ANY)
    return pl.pallas_call(
        functools.partial(kernel, n),
        out_shape=jax.ShapeDtypeStruct((rows, width), bf),
        in_specs=[vmem, vmem, vmem, anyw, anyw, anyw],
        out_specs=vmem,
        scratch_shapes=[
            pltpu.VMEM((2 * n * rows, width + LANES), bf),
            pltpu.VMEM((n * rows, width), bf),
            pltpu.VMEM((n * rows, width), bf),
            pltpu.VMEM((n * rows, width), bf),
            pltpu.VMEM((width, ffd), bf),
            pltpu.VMEM((width, ffd), bf),
            pltpu.VMEM((ffd, width), bf),
            pltpu.VMEM((4 * rows, ffd), bf),
            dma((3,)),
            dma((2, half + 1, 2)), dma((2, half + 1, 2)),
            dma((n, 2)), dma((n, 2)),
            dma((n, 2)), dma((n, 2)),
            dma((2, half + 1, 2)), dma((2, half + 1, 2)),
        ],
        compiler_params=pltpu.CompilerParams(
            collective_id=0, has_side_effects=True, vmem_limit_bytes=61 * 2 ** 20),
        cost_estimate=pl.CostEstimate(
            flops=12 * n * rows * width * ffd, bytes_accessed=6 * width * ffd, transcendentals=2 * n * rows * ffd),
    )(tokens, routes.T, gate_weights.T, w_gate, w_up, w_down)


def solution(mesh):
    spread = P(("groups", "dp", "expert"), None)
    return jax.shard_map(
        local,
        mesh=mesh,
        in_specs=(spread, spread, spread, P("expert", None, "dp"), P("expert", None, "dp"), P("expert", "dp", None)),
        out_specs=spread,
        check_vma=False,
    )
```
